32 devices in a mesh: replica: 16 (over z, x, core), group: 2 (over y).
Axes of the slice: x: 2, y: 2, z: 4, core: 2. Of those that a mesh axis runs over, the one named last changes fastest.
Arguments:
- tokens: bfloat16 [16384, 1024], P(('replica', 'group')), may hold values from -6 to 6
- cotangent: bfloat16 [16384, 1024], P(('replica', 'group')), may hold values from -6 to 6
- routes: int32 [16384, 8], P(('replica', 'group')), may hold values from 0 to 15, all different within a row; in each aligned block of 512 rows (0 to 511, 512 to 1023, ...) at most 320 rows name the same one
- first_gain: bfloat16 [1024], P('group'), may hold values from 0.5 to 1.5
- query_weight: bfloat16 [1024, 1024], P('group'), may hold values from -0.625 to 0.625
- key_weight: bfloat16 [1024, 512], P('group'), may hold values from -0.625 to 0.625
- value_weight: bfloat16 [1024, 512], P('group'), may hold values from -0.75 to 0.75
- output_weight: bfloat16 [1024, 1024], P('group'), may hold values from -0.75 to 0.75
- second_gain: bfloat16 [1024], P('group'), may hold values from 0.5 to 1.5
- router_weight: bfloat16 [1024, 16], P('group'), may hold values from -0.09375 to 0.09375
- gate_weight: bfloat16 [16, 1024, 512], P('group'), may hold values from -0.1875 to 0.1875
- up_weight: bfloat16 [16, 1024, 512], P('group'), may hold values from -0.1875 to 0.1875
- down_weight: bfloat16 [16, 512, 1024], P('group'), may hold values from -2 to 2
Outputs:
- layer_output: bfloat16 [16384, 1024], P(('replica', 'group'))
- tokens_grad: float32 [16384, 1024], P(('replica', 'group'))
- first_gain_grad: float32 [1024], P('group')
- query_grad: float32 [1024, 1024], P('group')
- key_grad: float32 [1024, 512], P('group')
- value_grad: float32 [1024, 512], P('group')
- output_grad: float32 [1024, 1024], P('group')
- second_gain_grad: float32 [1024], P('group')
- router_grad: float32 [1024, 16], P('group')
- gate_grad: float32 [16, 1024, 512], P('group')
- up_grad: float32 [16, 1024, 512], P('group')
- down_grad: float32 [16, 512, 1024], P('group')
The draws below stay inside these ranges and needn't reach their ends.
Inputs may be any that keep to these rules, and one draw needn't show every extreme that they name: `routes`: each row names 8 different experts. Within the tokens of one device no expert is named by more than 320 tokens, and in some device one expert is named by exactly 320.
All inputs are finite; a program needn't handle non-finite values.
Results may differ from the reference program's by a relative error of at most 0.02.
Values may be sent and summed in bfloat16 or wider, within the bound.
A program may use at most 320 MiB of HBM per device.

```python
import math
import jax
import jax.numpy as jnp
import numpy as np
from jax import lax

D = 1024
HQ = 16
KV = 8
HD = 64
FF = 512
E = 16
TOPK = 8
TOK_DEV = 512
GRP = 2
CAP = 320
TOKENS = 16384
N_REPLICA = 16
N_GROUP = 2


def block_levels(stream_key, extent, cuts, least, high):
    level = 1.0
    for dim, parts in cuts:
        draws = jax.random.uniform(jax.random.fold_in(jax.random.fold_in(stream_key, 6), dim), (parts,), jnp.float32, least / len(cuts), high / len(cuts))
        level = level * jnp.repeat(jnp.exp(draws), extent[dim] // parts).reshape((-1,) + (1,) * (len(extent) - 1 - dim))
    return level


def deal_out(key, own, number, rows, count, top, bound, slope):
    sequence = jax.random.permutation(key, count)
    crowded, usual = shares(count, rows * top, bound, slope, True), shares(count, rows * top, bound, slope, False)
    places = jnp.arange(count)

    def named(lengths, offset_by):
        used = int((lengths > 0).sum())
        fixed = max(1, used // 4)
        moved = fixed + (places - fixed + offset_by * (used - fixed)) % max(1, count - fixed)
        return jnp.zeros((count,), jnp.int32).at[sequence[jnp.where(places < fixed, places, moved)]].set(jnp.asarray(lengths, jnp.int32))

    lengths = jnp.where(number % 4 == 0, named(crowded, number // 4), named(usual, number - number // 4 - 1))
    mixed = jax.random.permutation(jax.random.fold_in(own, 3), count)
    giver, taker = mixed[0:count // 2 * 2:2], mixed[1:count // 2 * 2:2]
    slack = jnp.minimum(lengths[giver] - 1, bound - lengths[taker]) // 2
    slack = jnp.where((giver == sequence[0]) | (taker == sequence[0]) | (lengths[taker] == 0), 0, jnp.maximum(slack, 0))
    moved = jax.random.randint(jax.random.fold_in(own, 4), (count // 2,), 0, 1 << 20) % (slack + 1)
    lengths = lengths.at[giver].add(-moved).at[taker].add(moved)
    items = jnp.searchsorted(jnp.cumsum(lengths), jnp.arange(rows * top), side="right").astype(jnp.int32)
    grid = items.reshape(top, rows).T
    grid = grid[jax.random.permutation(jax.random.fold_in(own, 1), rows)]
    offset_by = jax.random.randint(jax.random.fold_in(own, 2), (rows, 1), 0, top)
    return jnp.take_along_axis(grid, (jnp.arange(top)[None, :] + offset_by) % top, axis=1)


def shares(count, total, most, slope, full):
    portions = [(1 << 20) // math.isqrt(standing ** slope) + 1 for standing in range(1, count + 1)]
    largest = most if full else min(most, max(-(-total // count), total * portions[0] // sum(portions)))
    least = 1 if total - largest >= count - 1 else 0
    holding, rest = [largest] + [least] * (count - 1), total - largest - least * (count - 1)
    while rest > 0:
        candidates = [i for i in range(1, count) if holding[i] < largest] or [i for i in range(1, count) if holding[i] < most]
        whole, left = sum([portions[i] for i in candidates]), rest
        for i in candidates:
            extra = min(most - holding[i], max(1, left * portions[i] // whole), rest)
            holding[i] = holding[i] + extra
            rest = rest - extra
    return np.array(holding)


def bell_draw(rng, dims, spread, most, pieces=(), held_as=jnp.bfloat16):
    values = spread * jax.random.normal(rng, dims, jnp.float32)
    if pieces:
        values = values * block_levels(rng, dims, pieces, -0.22, 0.18)
    return jnp.clip(values, -most, most).astype(held_as)


def setup_inputs(seed: int = 0) -> dict:
    splits = jax.random.split(jax.random.key(seed), 14)
    tokens = bell_draw(splits[0], (TOKENS, D), 1.0, 6.0, ((0, 32),))
    cotangent = bell_draw(splits[1], (TOKENS, D), 1.0, 6.0, ((0, 32),))
    routes_keys = jax.random.split(jax.random.fold_in(splits[2], 1), TOKENS // TOK_DEV)
    routes_turns = jax.random.permutation(jax.random.fold_in(splits[2], 3), TOKENS // TOK_DEV)
    routes = jax.vmap(lambda own, number: deal_out(jax.random.fold_in(splits[2], 2), own, number, TOK_DEV, E, TOPK, CAP, 0))(routes_keys, routes_turns).reshape((TOKENS, TOPK))
    first_gain = jnp.clip(1.0 + 0.1 * jax.random.normal(splits[3], (D,), jnp.float32), 0.5, 1.5).astype(jnp.bfloat16)
    query_weight = bell_draw(splits[4], (D, HQ * HD), (D // 12) ** -0.5, 0.625, ((0, 2),))
    key_weight = bell_draw(splits[5], (D, KV * HD), (D // 12) ** -0.5, 0.625, ((0, 2),))
    value_weight = bell_draw(splits[6], (D, KV * HD), (D // 16) ** -0.5, 0.75, ((0, 2),))
    output_weight = bell_draw(splits[7], (HQ * HD, D), (HQ * HD // 16) ** -0.5, 0.75, ((0, 2),))
    second_gain = jnp.clip(1.0 + 0.1 * jax.random.normal(splits[8], (D,), jnp.float32), 0.5, 1.5).astype(jnp.bfloat16)
    router_weight = bell_draw(splits[9], (D, E), (4 * D) ** -0.5, 0.09375, ((0, 2),))
    gate_weight = bell_draw(splits[10], (E, D, FF), D ** -0.5, 0.1875, ((0, 2),))
    up_weight = bell_draw(splits[11], (E, D, FF), D ** -0.5, 0.1875, ((0, 2),))
    down_weight = bell_draw(splits[12], (E, FF, D), (FF // 64 + 1) ** -0.5, 2.0, ((0, 2),))
    return {"tokens": tokens, "cotangent": cotangent, "routes": routes, "first_gain": first_gain, "query_weight": query_weight, "key_weight": key_weight, "value_weight": value_weight, "output_weight": output_weight, "second_gain": second_gain, "router_weight": router_weight, "gate_weight": gate_weight, "up_weight": up_weight, "down_weight": down_weight}


norm_eps = 1e-06
residual_scale = 0.22
score_scale = 0.015625
rope_base = 10000.0
masked_value = -1e+30

@jax.custom_vjp
def low(v):
    return lax.optimization_barrier(v.astype(jnp.bfloat16)).astype(jnp.float32)

@jax.custom_vjp
def low_back(v):
    return v

def low_keep(v):
    return (low(v), None)

def low_pass(kept, grad):
    return (grad,)

def back_keep(v):
    return (v, None)

def back_low(kept, grad):
    return (low(grad),)
low.defvjp(low_keep, low_pass)
low_back.defvjp(back_keep, back_low)

def matmul(factor_left, factor_right):
    return jnp.dot(factor_left, factor_right, precision=lax.Precision.HIGHEST, preferred_element_type=jnp.float32)

def softmax_rows(scores):
    shifted = jnp.exp(scores - lax.optimization_barrier(jnp.max(scores, axis=-1, keepdims=True)))
    return shifted / lax.optimization_barrier(jnp.sum(shifted, axis=-1, keepdims=True))

def rope_tables(length):
    positions = jnp.arange(length, dtype=jnp.float32)
    inverse = rope_base ** (-jnp.arange(0, HD, 2, dtype=jnp.float32) / HD)
    angles = positions[:, None] * inverse[None, :]
    cosine_table = jnp.cos(angles)
    sine_table = jnp.sin(angles)
    return (jnp.concatenate([cosine_table, cosine_table], -1), jnp.concatenate([sine_table, sine_table], -1))

def rotate(values, cosine_table, sine_table):
    half_width = values.shape[-1] // 2
    turned = jnp.concatenate([-values[..., half_width:], values[..., :half_width]], -1)
    return values * cosine_table[:, None, :] + turned * sine_table[:, None, :]

def slot_table(routes_seq):
    flat_routes = routes_seq.reshape(-1)
    one_hot = (flat_routes[:, None] == jnp.arange(E, dtype=jnp.int32)[None, :]).astype(jnp.int32)
    earlier = jnp.cumsum(one_hot, axis=0) - one_hot
    position = lax.optimization_barrier(jnp.sum(earlier * one_hot, axis=1))
    slot_of = flat_routes * CAP + position
    entries = flat_routes.shape[0]
    source = jnp.full((E * CAP,), entries, jnp.int32).at[slot_of].set(jnp.arange(entries, dtype=jnp.int32))
    return (slot_of, source)

def layer(tokens_seq, routes_seq, params):
    first_gain, query_weight, key_weight, value_weight, output_weight, second_gain, router_weight, gate_weight, up_weight, down_weight = params
    length = tokens_seq.shape[0]
    width = tokens_seq.shape[1]
    cosine_table, sine_table = rope_tables(length)
    scale_one = lax.rsqrt(lax.optimization_barrier(jnp.mean(tokens_seq * tokens_seq, axis=-1, keepdims=True)) + norm_eps)
    normed_one = low(tokens_seq * scale_one * first_gain)
    query_pre = low_back(matmul(normed_one, query_weight)).reshape(length, HQ, HD)
    queries = low(rotate(query_pre, cosine_table, sine_table))
    key_pre = low_back(matmul(normed_one, key_weight)).reshape(length, KV, HD)
    key_rows = low(rotate(key_pre, cosine_table, sine_table))
    values = low(low_back(matmul(normed_one, value_weight))).reshape(length, KV, HD)
    keys_wide = jnp.repeat(key_rows, GRP, axis=1)
    values_wide = jnp.repeat(values, GRP, axis=1)
    scores = low_back(jnp.einsum('shd,thd->hst', queries, keys_wide, precision=lax.Precision.HIGHEST) * score_scale)
    causal = jnp.arange(length)[:, None] >= jnp.arange(length)[None, :]
    scores = jnp.where(causal[None], scores, masked_value)
    probability = low(softmax_rows(scores))
    attention_mix = jnp.einsum('hst,thd->shd', probability, values_wide, precision=lax.Precision.HIGHEST)
    attention_mix = low(low_back(attention_mix.reshape(length, HQ * HD)))
    resid = tokens_seq + residual_scale * low_back(matmul(attention_mix, output_weight))
    scale_two = lax.rsqrt(lax.optimization_barrier(jnp.mean(resid * resid, axis=-1, keepdims=True)) + norm_eps)
    normed_two = low(resid * scale_two * second_gain)
    logits = low_back(matmul(normed_two, router_weight))
    route_gates = softmax_rows(jnp.take_along_axis(logits, routes_seq, axis=1))
    slot_of, source = slot_table(routes_seq)
    padded = jnp.concatenate([normed_two, jnp.zeros((1, width), normed_two.dtype)], 0)
    expert_in = padded[source // TOPK].reshape(E, CAP, width)
    gate_pre = low_back(jnp.einsum('ecd,edf->ecf', expert_in, gate_weight, precision=lax.Precision.HIGHEST))
    up_pre = low_back(jnp.einsum('ecd,edf->ecf', expert_in, up_weight, precision=lax.Precision.HIGHEST))
    hidden = low(jax.nn.silu(gate_pre) * up_pre)
    expert_out = low(low_back(jnp.einsum('ecf,efd->ecd', hidden, down_weight, precision=lax.Precision.HIGHEST)))
    picked = expert_out.reshape(E * CAP, width)[slot_of].reshape(length, TOPK, width)
    return resid + residual_scale * lax.optimization_barrier(jnp.sum(route_gates[:, :, None] * picked, axis=1))

def reference(tokens, cotangent, routes, first_gain, query_weight, key_weight, value_weight, output_weight, second_gain, router_weight, gate_weight, up_weight, down_weight):
    sequences = N_REPLICA * N_GROUP
    params = (first_gain.astype(jnp.float32), query_weight.astype(jnp.float32), key_weight.astype(jnp.float32), value_weight.astype(jnp.float32), output_weight.astype(jnp.float32), second_gain.astype(jnp.float32), router_weight.astype(jnp.float32), gate_weight.astype(jnp.float32), up_weight.astype(jnp.float32), down_weight.astype(jnp.float32))
    tokens_all = tokens.astype(jnp.float32).reshape(sequences, TOK_DEV, D)
    routes_all = routes.reshape(sequences, TOK_DEV, TOPK)
    layer_step = jax.checkpoint(layer)

    def forward(tokens_in, params_in):
        return lax.map(lambda paired: layer_step(paired[0], paired[1], params_in), (tokens_in, routes_all))
    outputs, pullback = jax.vjp(forward, tokens_all, params)
    tokens_back, params_back = pullback(cotangent.astype(jnp.float32).reshape(sequences, TOK_DEV, D))
    return (outputs.reshape(TOKENS, D).astype(jnp.bfloat16), tokens_back.reshape(TOKENS, D), params_back[0], params_back[1], params_back[2], params_back[3], params_back[4], params_back[5], params_back[6], params_back[7], params_back[8], params_back[9])
```

```python
import functools

import jax
import jax.numpy as jnp
from jax import lax
from jax.sharding import PartitionSpec as P

HQ = 16
KV = 8
HD = 64
E = 16
GRP = 2


norm_eps = 1e-06
residual_scale = 0.22
score_scale = 0.015625
rope_base = 10000.0
masked_value = -1e30


def rope_tables(length):
    positions = jnp.arange(length, dtype=jnp.float32)
    inverse = rope_base ** (-jnp.arange(0, HD, 2, dtype=jnp.float32) / HD)
    angles = positions[:, None] * inverse[None, :]
    cosine_table = jnp.cos(angles)
    sine_table = jnp.sin(angles)
    return (
        jnp.concatenate([cosine_table, cosine_table], -1),
        jnp.concatenate([sine_table, sine_table], -1),
    )


def rotate(values, cosine_table, sine_table):
    half_width = values.shape[-1] // 2
    turned = jnp.concatenate([-values[..., half_width:], values[..., :half_width]], -1)
    return values * cosine_table[:, None, :] + turned * sine_table[:, None, :]


def rotate_back(grads, cosine_table, sine_table):
    half_width = grads.shape[-1] // 2
    with_sine = grads * sine_table[:, None, :]
    turned = jnp.concatenate([with_sine[..., half_width:], -with_sine[..., :half_width]], -1)
    return grads * cosine_table[:, None, :] + turned


def swap(values, axis, size, bit):
    return lax.ppermute(values, axis, [(i, i ^ bit) for i in range(size)])


def side_of(axis, bit):
    return (lax.axis_index(axis) // bit) % 2


def bits_of(size):
    return [1 << place for place in range(size.bit_length() - 1)]


def fold(values, dim, axis, size, bit):
    side = side_of(axis, bit)
    half = values.shape[dim] // 2
    send = lax.dynamic_slice_in_dim(values, (1 - side) * half, half, dim)
    keep = lax.dynamic_slice_in_dim(values, side * half, half, dim)
    received = swap(send, axis, size, bit)
    return (keep.astype(jnp.float32) + received.astype(jnp.float32)).astype(jnp.bfloat16)


def unfold(values, dim, axis, size, bit, kept=jnp.bfloat16):
    side = side_of(axis, bit)
    other = swap(values, axis, size, bit).astype(kept)
    values = values.astype(kept)
    lower = jnp.where(side == 0, values, other)
    upper = jnp.where(side == 0, other, values)
    return jnp.concatenate([lower, upper], dim)


def group_gather(values, groups):
    for bit in bits_of(groups):
        values = unfold(values, 0, "group", groups, bit, values.dtype)
    return values


def group_scatter(values, groups):
    for bit in reversed(bits_of(groups)):
        values = fold(values, 0, "group", groups, bit)
    return values


def gather_rows(values, replicas, groups):
    rows, columns = values.shape
    half = rows // 2
    part = lax.dynamic_slice_in_dim(values, side_of("replica", 1) * half, half, 0)
    part = group_gather(part[None], groups)
    return unfold(part, 1, "replica", replicas, 1).reshape(groups * rows, columns)


def replica_sum(values, replicas, dim):
    for bit in bits_of(replicas):
        values = fold(values, dim, "replica", replicas, bit)
    for bit in reversed(bits_of(replicas)):
        kept = jnp.float32 if bit == 1 else jnp.bfloat16
        values = unfold(values, dim, "replica", replicas, bit, kept)
    return values


def own_rows_sum(values, replicas, groups):
    rows, columns = values.shape
    values = values.astype(jnp.bfloat16).reshape(groups, rows // groups, columns)
    values = fold(values, 1, "replica", replicas, 1)
    values = group_scatter(values, groups)
    for bit in bits_of(replicas)[1:]:
        values = fold(values, 1, "replica", replicas, bit)
    for bit in reversed(bits_of(replicas)):
        values = unfold(values, 1, "replica", replicas, bit)
    return values[0].astype(jnp.float32)


def expert_sum(values, replicas):
    shape = values.shape
    flat = values.astype(jnp.bfloat16).reshape(shape[0] * shape[1], shape[2])
    return replica_sum(flat, replicas, 0).reshape(shape)


def head_slices(queries, key_rows, values, group_index, length):
    query_block = lax.dynamic_slice_in_dim(queries, group_index * GRP * HD, GRP * HD, 1).reshape(
        length, GRP, HD
    )
    key_block = lax.dynamic_slice_in_dim(key_rows, group_index * HD, HD, 1)
    value_block = lax.dynamic_slice_in_dim(values, group_index * HD, HD, 1)
    return (query_block, key_block, value_block)


def attend_forward(queries, key_rows, values, causal):
    length = queries.shape[0]

    def one_group(group_index):
        query_block, key_block, value_block = head_slices(
            queries, key_rows, values, group_index, length
        )
        scores = (
            jnp.einsum("sgd,td->gst", query_block, key_block, preferred_element_type=jnp.float32)
            * score_scale
        )
        scores = jnp.where(causal[None], scores, masked_value)
        row_peak = jnp.max(scores, axis=-1, keepdims=True)
        exponent = jnp.exp(scores - row_peak)
        row_total = jnp.sum(exponent, axis=-1, keepdims=True)
        probability = (exponent / row_total).astype(jnp.bfloat16)
        block_mix = jnp.einsum(
            "gst,td->sgd", probability, value_block, preferred_element_type=jnp.float32
        )
        return (block_mix.reshape(length, GRP * HD), (row_peak + jnp.log(row_total))[..., 0])

    blocks, log_sums = lax.map(one_group, jnp.arange(KV, dtype=jnp.int32))
    return (blocks.transpose(1, 0, 2).reshape(length, HQ * HD), log_sums)


def attend_backward(queries, key_rows, values, grad_mix, log_sums, causal):
    length = queries.shape[0]

    def one_group(paired):
        group_index, group_sums = paired
        query_block, key_block, value_block = head_slices(
            queries, key_rows, values, group_index, length
        )
        grad_block = lax.dynamic_slice_in_dim(
            grad_mix, group_index * GRP * HD, GRP * HD, 1
        ).reshape(length, GRP, HD)
        scores = (
            jnp.einsum("sgd,td->gst", query_block, key_block, preferred_element_type=jnp.float32)
            * score_scale
        )
        scores = jnp.where(causal[None], scores, masked_value)
        probability = jnp.exp(scores - group_sums[..., None])
        rounded = probability.astype(jnp.bfloat16)
        grad_prob = jnp.einsum(
            "sgd,td->gst", grad_block, value_block, preferred_element_type=jnp.float32
        )
        grad_scores = probability * (
            grad_prob - jnp.sum(probability * grad_prob, axis=-1, keepdims=True)
        )
        grad_scores = grad_scores.astype(jnp.bfloat16)
        grad_query = (
            jnp.einsum("gst,td->sgd", grad_scores, key_block, preferred_element_type=jnp.float32)
            * score_scale
        )
        grad_key = (
            jnp.einsum("gst,sgd->td", grad_scores, query_block, preferred_element_type=jnp.float32)
            * score_scale
        )
        grad_value = jnp.einsum(
            "gst,sgd->td", rounded, grad_block, preferred_element_type=jnp.float32
        )
        return (grad_query.reshape(length, GRP * HD), grad_key, grad_value)

    query_parts, key_parts, value_parts = lax.map(
        one_group, (jnp.arange(KV, dtype=jnp.int32), log_sums)
    )
    return (
        query_parts.transpose(1, 0, 2).reshape(length, HQ * HD),
        key_parts.transpose(1, 0, 2).reshape(length, KV * HD),
        value_parts.transpose(1, 0, 2).reshape(length, KV * HD),
    )


def shards(
    replicas,
    groups,
    tokens,
    cotangent,
    routes,
    first_gain,
    query_weight,
    key_weight,
    value_weight,
    output_weight,
    second_gain,
    router_weight,
    gate_weight,
    up_weight,
    down_weight,
):
    length = tokens.shape[0]
    local_experts = gate_weight.shape[0]
    query_width = query_weight.shape[1]
    key_width = key_weight.shape[1]
    spare = 128 - E - 2
    wide = jnp.concatenate([query_weight, key_weight, value_weight], 1)
    late = jnp.concatenate(
        [
            output_weight,
            router_weight,
            second_gain[:, None],
            first_gain[:, None],
            jnp.zeros((output_weight.shape[0], spare), jnp.bfloat16),
        ],
        1,
    )
    gain_one = group_gather(first_gain, groups)
    wide_full = gather_rows(wide, replicas, groups)
    late_full = gather_rows(late, replicas, groups)
    routes_all = group_gather(routes, groups)
    cotangent_all = group_gather(cotangent, groups)
    output_width = output_weight.shape[1]
    output_full = late_full[:, :output_width]
    router_full = late_full[:, output_width : output_width + E]
    gain_two = late_full[:, output_width + E]
    tokens_float = tokens.astype(jnp.float32)
    scale_one = lax.rsqrt(jnp.mean(tokens_float * tokens_float, axis=-1, keepdims=True) + norm_eps)
    normed_one = (tokens_float * scale_one * gain_one.astype(jnp.float32)).astype(jnp.bfloat16)
    cosine_table, sine_table = rope_tables(length)
    projected = jnp.dot(normed_one, wide_full, preferred_element_type=jnp.float32)
    query_pre = projected[:, :query_width].reshape(length, HQ, HD)
    queries = (
        rotate(query_pre, cosine_table, sine_table).astype(jnp.bfloat16).reshape(length, HQ * HD)
    )
    key_pre = projected[:, query_width : query_width + key_width].reshape(length, KV, HD)
    key_rows = (
        rotate(key_pre, cosine_table, sine_table).astype(jnp.bfloat16).reshape(length, KV * HD)
    )
    values = projected[:, query_width + key_width :].astype(jnp.bfloat16)
    causal = jnp.arange(length)[:, None] >= jnp.arange(length)[None, :]
    attention_raw, log_sums = attend_forward(queries, key_rows, values, causal)
    attention_mix = attention_raw.astype(jnp.bfloat16)
    attention_out = jnp.dot(attention_mix, output_full, preferred_element_type=jnp.float32)
    resid = tokens_float + residual_scale * attention_out
    scale_two = lax.rsqrt(jnp.mean(resid * resid, axis=-1, keepdims=True) + norm_eps)
    normed_two = (resid * scale_two * gain_two.astype(jnp.float32)).astype(jnp.bfloat16)

    normed_all = group_gather(normed_two, groups)
    logits = jnp.dot(normed_all, router_full, preferred_element_type=jnp.float32)
    chosen = jnp.any(
        routes_all[:, :, None] == jnp.arange(E, dtype=jnp.int32)[None, None, :], axis=1
    )
    shown = jnp.where(chosen, logits, -jnp.inf)
    gates = jax.nn.softmax(shown, axis=-1)
    first_expert = lax.axis_index("group") * local_experts
    gates_local = lax.dynamic_slice_in_dim(gates, first_expert, local_experts, 1)
    gates_column = gates_local.T[:, :, None]

    gate_pre = jnp.einsum(
        "td,edf->etf", normed_all, gate_weight, preferred_element_type=jnp.float32
    )
    up_pre = jnp.einsum("td,edf->etf", normed_all, up_weight, preferred_element_type=jnp.float32)
    sigmoid_gate = jax.nn.sigmoid(gate_pre)
    swish_gate = gate_pre * sigmoid_gate
    hidden = swish_gate * up_pre
    hidden_gated = (gates_column * hidden).astype(jnp.bfloat16)
    grad_hidden_plain = residual_scale * jnp.einsum(
        "td,efd->etf", cotangent_all, down_weight, preferred_element_type=jnp.float32
    )
    down_part = residual_scale * jnp.einsum(
        "etf,td->efd", hidden_gated, cotangent_all, preferred_element_type=jnp.float32
    )
    down_grad = expert_sum(down_part, replicas)
    grad_gates = jnp.sum(grad_hidden_plain * hidden, axis=-1).T
    grad_hidden = gates_column * grad_hidden_plain
    grad_gate = (
        grad_hidden * up_pre * sigmoid_gate * (1.0 + gate_pre * (1.0 - sigmoid_gate))
    ).astype(jnp.bfloat16)
    grad_up = (grad_hidden * swish_gate).astype(jnp.bfloat16)
    gate_part = jnp.einsum(
        "td,etf->edf", normed_all, grad_gate, preferred_element_type=jnp.float32
    )
    gate_grad = expert_sum(gate_part, replicas)
    up_part = jnp.einsum("td,etf->edf", normed_all, grad_up, preferred_element_type=jnp.float32)
    up_grad = expert_sum(up_part, replicas)
    moe_part = jnp.einsum(
        "etf,efd->td", hidden_gated, down_weight, preferred_element_type=jnp.float32
    )
    moe_out = group_scatter(moe_part.astype(jnp.bfloat16), groups).astype(jnp.float32)
    layer_output = (resid + residual_scale * moe_out).astype(jnp.bfloat16)

    grad_chosen = gates_local * grad_gates
    grad_logits = lax.dynamic_update_slice_in_dim(
        jnp.zeros_like(gates), grad_chosen, first_expert, 1
    ) - gates * jnp.sum(grad_chosen, axis=-1, keepdims=True)
    grad_logits = grad_logits.astype(jnp.bfloat16)
    router_part = jnp.einsum(
        "sd,se->de", normed_all, grad_logits, preferred_element_type=jnp.float32
    )
    grad_normed_part = (
        jnp.einsum("etf,edf->td", grad_gate, gate_weight, preferred_element_type=jnp.float32)
        + jnp.einsum("etf,edf->td", grad_up, up_weight, preferred_element_type=jnp.float32)
        + jnp.einsum("se,de->sd", grad_logits, router_full, preferred_element_type=jnp.float32)
    )
    grad_normed_two = group_scatter(grad_normed_part.astype(jnp.bfloat16), groups).astype(
        jnp.float32
    )
    grad_out = cotangent.astype(jnp.float32)
    second_part = jnp.sum(grad_normed_two * resid * scale_two, axis=0)
    weighted_two = grad_normed_two * gain_two.astype(jnp.float32)
    grad_resid = (
        grad_out
        + scale_two * weighted_two
        - resid * scale_two**3 * jnp.mean(weighted_two * resid, axis=-1, keepdims=True)
    )
    grad_attention = (residual_scale * grad_resid).astype(jnp.bfloat16)
    output_part = jnp.einsum(
        "sk,sd->kd", attention_mix, grad_attention, preferred_element_type=jnp.float32
    )
    early_sum = own_rows_sum(
        jnp.concatenate(
            [
                output_part,
                router_part,
                second_part[:, None],
                jnp.zeros((output_part.shape[0], spare + 1), jnp.float32),
            ],
            1,
        ),
        replicas,
        groups,
    )
    grad_mix = jnp.einsum(
        "sd,kd->sk", grad_attention, output_full, preferred_element_type=jnp.float32
    ).astype(jnp.bfloat16)
    grad_query_rot, grad_key_rot, grad_value_raw = attend_backward(
        queries, key_rows, values, grad_mix, log_sums, causal
    )
    grad_query_pre = rotate_back(grad_query_rot.reshape(length, HQ, HD), cosine_table, sine_table)
    grad_key_pre = rotate_back(grad_key_rot.reshape(length, KV, HD), cosine_table, sine_table)
    grad_wide = jnp.concatenate(
        [
            grad_query_pre.reshape(length, HQ * HD).astype(jnp.bfloat16),
            grad_key_pre.reshape(length, KV * HD).astype(jnp.bfloat16),
            grad_value_raw.astype(jnp.bfloat16),
        ],
        1,
    )
    grad_normed_one = jnp.einsum(
        "sk,dk->sd", grad_wide, wide_full, preferred_element_type=jnp.float32
    )
    first_part = jnp.sum(grad_normed_one * tokens_float * scale_one, axis=0)
    wide_part = jnp.einsum("sd,sk->dk", normed_one, grad_wide, preferred_element_type=jnp.float32)
    late_sum = own_rows_sum(
        jnp.concatenate(
            [
                wide_part,
                first_part[:, None],
                jnp.zeros((wide_part.shape[0], 127), jnp.float32),
            ],
            1,
        ),
        replicas,
        groups,
    )
    weighted_one = grad_normed_one * gain_one.astype(jnp.float32)
    tokens_grad = (
        grad_resid
        + scale_one * weighted_one
        - tokens_float
        * scale_one**3
        * jnp.mean(weighted_one * tokens_float, axis=-1, keepdims=True)
    )
    wide_width = wide.shape[1]
    return (
        layer_output,
        tokens_grad,
        late_sum[:, wide_width],
        late_sum[:, :query_width],
        late_sum[:, query_width : query_width + key_width],
        late_sum[:, query_width + key_width : wide_width],
        early_sum[:, :output_width],
        early_sum[:, output_width + E],
        early_sum[:, output_width : output_width + E],
        gate_grad,
        up_grad,
        down_grad,
    )


def solution(mesh):
    return jax.shard_map(
        functools.partial(shards, mesh.shape["replica"], mesh.shape["group"]),
        mesh=mesh,
        in_specs=(
            P(("replica", "group"), None),
            P(("replica", "group"), None),
            P(("replica", "group"), None),
            P("group"),
            P("group", None),
            P("group", None),
            P("group", None),
            P("group", None),
            P("group"),
            P("group", None),
            P("group", None, None),
            P("group", None, None),
            P("group", None, None),
        ),
        out_specs=(
            P(("replica", "group"), None),
            P(("replica", "group"), None),
            P("group"),
            P("group", None),
            P("group", None),
            P("group", None),
            P("group", None),
            P("group"),
            P("group", None),
            P("group", None, None),
            P("group", None, None),
            P("group", None, None),
        ),
        check_vma=False,
    )
```

```python
import functools

import jax
import jax.numpy as jnp
from jax import lax
from jax.experimental import pallas as pl
from jax.experimental.pallas import tpu as pltpu
from jax.sharding import PartitionSpec as P

HQ = 16
KV = 8
HD = 64
E = 16
GRP = 2


norm_eps = 1e-06
residual_scale = 0.22
score_scale = 0.015625
rope_base = 10000.0
masked_value = -1e30


def rope_tables(length):
    positions = jnp.arange(length, dtype=jnp.float32)
    inverse = rope_base ** (-jnp.arange(0, HD, 2, dtype=jnp.float32) / HD)
    angles = positions[:, None] * inverse[None, :]
    cosine_table = jnp.cos(angles)
    sine_table = jnp.sin(angles)
    return (
        jnp.concatenate([cosine_table, cosine_table], -1),
        jnp.concatenate([sine_table, sine_table], -1),
    )


def swap(values, axis, size, bit):
    return lax.ppermute(values, axis, [(i, i ^ bit) for i in range(size)])


def side_of(axis, bit):
    return (lax.axis_index(axis) // bit) % 2


def bits_of(size):
    return [1 << place for place in range(size.bit_length() - 1)]


def fold(values, dim, axis, size, bit):
    side = side_of(axis, bit)
    half = values.shape[dim] // 2
    send = lax.dynamic_slice_in_dim(values, (1 - side) * half, half, dim)
    keep = lax.dynamic_slice_in_dim(values, side * half, half, dim)
    received = swap(send, axis, size, bit)
    return (keep.astype(jnp.float32) + received.astype(jnp.float32)).astype(jnp.bfloat16)


def unfold(values, dim, axis, size, bit, kept=jnp.bfloat16):
    side = side_of(axis, bit)
    other = swap(values, axis, size, bit).astype(kept)
    values = values.astype(kept)
    lower = jnp.where(side == 0, values, other)
    upper = jnp.where(side == 0, other, values)
    return jnp.concatenate([lower, upper], dim)


def group_gather(values, groups):
    for bit in bits_of(groups):
        values = unfold(values, 0, "group", groups, bit, values.dtype)
    return values


def group_scatter(values, groups):
    for bit in reversed(bits_of(groups)):
        values = fold(values, 0, "group", groups, bit)
    return values


def gather_rows(values, replicas, groups):
    rows, columns = values.shape
    half = rows // 2
    part = lax.dynamic_slice_in_dim(values, side_of("replica", 1) * half, half, 0)
    part = group_gather(part[None], groups)
    return unfold(part, 1, "replica", replicas, 1).reshape(groups * rows, columns)


def join_kernel(side_ref, own_ref, other_ref, out_ref):
    own_here = pl.program_id(0) // (pl.num_programs(0) // 2) == side_ref[0]

    @pl.when(own_here)
    def _():
        out_ref[...] = own_ref[...].astype(jnp.float32)

    @pl.when(jnp.logical_not(own_here))
    def _():
        out_ref[...] = other_ref[...].astype(jnp.float32)


def join_halves(values, replicas):
    rows, columns = values.shape
    other = swap(values, "replica", replicas, 1)
    parts = 4
    half_spec = pl.BlockSpec((rows // parts, columns), lambda i, side: (i % parts, 0))
    return pl.pallas_call(
        join_kernel,
        grid_spec=pltpu.PrefetchScalarGridSpec(
            num_scalar_prefetch=1,
            grid=(2 * parts,),
            in_specs=[half_spec, half_spec],
            out_specs=pl.BlockSpec((rows // parts, columns), lambda i, side: (i, 0)),
        ),
        out_shape=jax.ShapeDtypeStruct((2 * rows, columns), jnp.float32),
        compiler_params=pltpu.CompilerParams(vmem_limit_bytes=24 * 1024 * 1024),
        cost_estimate=pl.CostEstimate(
            flops=0, bytes_accessed=16 * rows * columns, transcendentals=0
        ),
    )(side_of("replica", 1).astype(jnp.int32).reshape(1), values, other)


def sum_step(values, replicas, place, swapped=False):
    bits = bits_of(replicas)
    if swapped:
        bits = bits[:1] + bits[2:] + bits[1:2]
    if place < len(bits):
        return fold(values, 0, "replica", replicas, bits[place])
    if place == 2 * len(bits) - 1:
        return join_halves(values, replicas)
    return unfold(values, 0, "replica", replicas, bits[2 * len(bits) - 1 - place])


def flat_rows(values):
    return values.astype(jnp.bfloat16).reshape(-1, values.shape[-1])


def small_step(values, replicas, groups, place):
    bits = bits_of(replicas)
    if place == 1:
        return group_scatter(values, groups)
    place = place if place == 0 else place - 1
    if place < len(bits):
        return fold(values, 1, "replica", replicas, bits[place])
    return unfold(values, 1, "replica", replicas, bits[2 * len(bits) - 1 - place])


def lane_side(width):
    return lax.broadcasted_iota(jnp.int32, (1, width), 1) // HD % 2


def turned_lanes(block):
    first = lax.broadcasted_iota(jnp.int32, (1, 2 * HD), 1) % HD < HD // 2
    return jnp.where(first, -pltpu.roll(block, 3 * HD // 2, 1), pltpu.roll(block, HD // 2, 1))


def turned_back(block):
    first = lax.broadcasted_iota(jnp.int32, (1, 2 * HD), 1) % HD < HD // 2
    return jnp.where(first, pltpu.roll(block, 3 * HD // 2, 1), -pltpu.roll(block, HD // 2, 1))


def both_sides(block, head):
    own = jnp.where(lane_side(2 * HD) == head, block, 0.0)
    moved = pltpu.roll(own, HD, 1)
    pair = (own, moved) if head == 0 else (moved, own)
    return [part.astype(jnp.bfloat16) for part in pair]


def lanes_dot(left, right):
    return lax.dot_general(
        left, right, (((1,), (1,)), ((), ())), preferred_element_type=jnp.float32
    )


def rows_dot(left, right):
    return lax.dot_general(
        left, right, (((0,), (0,)), ((), ())), preferred_element_type=jnp.float32
    )


def forward_kernel(query_ref, key_ref, value_ref, cos_ref, sin_ref, mix_ref):
    cosine, sine = cos_ref[...], sin_ref[...]
    length = query_ref.shape[0]
    step = min(256, length)
    key_raw = key_ref[...]
    key_block = (key_raw * cosine + turned_lanes(key_raw) * sine).astype(jnp.bfloat16)
    key_block = key_block.astype(jnp.float32) * score_scale
    value_block = value_ref[...]
    for head in range(2):
        lanes = slice(2 * HD * head, 2 * HD * (head + 1))
        query_raw = query_ref[:, lanes]
        query_pair = (query_raw * cosine + turned_lanes(query_raw) * sine).astype(jnp.bfloat16)
        key_sides = both_sides(key_block, head)
        value_sides = both_sides(value_block, head)
        for start in range(0, length, step):
            end = start + step
            row = lax.broadcasted_iota(jnp.int32, (step, end), 0) + start
            column = lax.broadcasted_iota(jnp.int32, (step, end), 1)
            total = None
            for key_side, value_side in zip(key_sides, value_sides):
                scores = lanes_dot(query_pair[start:end], key_side[:end])
                scores = jnp.where(row >= column, scores, masked_value)
                exponent = jnp.exp(scores - jnp.max(scores, axis=1, keepdims=True))
                inverse = 1.0 / jnp.sum(exponent, axis=1, keepdims=True)
                rounded = (exponent * inverse).astype(jnp.bfloat16)
                part = jnp.dot(rounded, value_side[:end], preferred_element_type=jnp.float32)
                total = part if total is None else total + part
            mix_ref[start:end, lanes] = total.astype(jnp.bfloat16)


def backward_kernel(
    query_ref, key_ref, value_ref, grad_ref, cos_ref, sin_ref, dquery_ref, dkey_ref, dvalue_ref
):
    cosine, sine = cos_ref[...], sin_ref[...]
    length = query_ref.shape[0]
    step = min(256, length)
    key_raw = key_ref[...]
    key_block = (key_raw * cosine + turned_lanes(key_raw) * sine).astype(jnp.bfloat16)
    key_block = key_block.astype(jnp.float32) * score_scale
    value_block = value_ref[...]
    side_lane = lane_side(2 * HD)
    key_total, value_total = None, None
    for head in range(2):
        lanes = slice(2 * HD * head, 2 * HD * (head + 1))
        query_raw = query_ref[:, lanes]
        query_pair = (query_raw * cosine + turned_lanes(query_raw) * sine).astype(jnp.bfloat16)
        grad_pair = grad_ref[:, lanes]
        key_sides = both_sides(key_block, head)
        value_sides = both_sides(value_block, head)
        query_grads = [0.0 for _ in range(0, length, step)]
        for side in range(2):
            key_side, value_side = key_sides[side], value_sides[side]
            key_grads = [0.0 for _ in range(0, length, step)]
            value_grads = [0.0 for _ in range(0, length, step)]
            for place in range(length // step):
                start = place * step
                end = start + step
                column = lax.broadcasted_iota(jnp.int32, (end, step), 0)
                row = lax.broadcasted_iota(jnp.int32, (end, step), 1) + start
                scores = lanes_dot(key_side[:end], query_pair[start:end])
                scores = jnp.where(row >= column, scores, masked_value)
                exponent = jnp.exp(scores - jnp.max(scores, axis=0, keepdims=True))
                probability = exponent * (1.0 / jnp.sum(exponent, axis=0, keepdims=True))
                grad_prob = lanes_dot(value_side[:end], grad_pair[start:end])
                inner = jnp.sum(probability * grad_prob, axis=0, keepdims=True)
                grad_scores = (probability * (grad_prob - inner)).astype(jnp.bfloat16)
                rounded = probability.astype(jnp.bfloat16)
                query_grads[place] += rows_dot(grad_scores, key_side[:end])
                key_part = jnp.dot(
                    grad_scores, query_pair[start:end], preferred_element_type=jnp.float32
                )
                value_part = jnp.dot(
                    rounded, grad_pair[start:end], preferred_element_type=jnp.float32
                )
                for other in range(place + 1):
                    rows = slice(other * step, (other + 1) * step)
                    key_grads[other] += key_part[rows]
                    value_grads[other] += value_part[rows]
            key_own = jnp.where(side_lane == side, jnp.concatenate(key_grads, 0), 0.0)
            value_own = jnp.where(side_lane == side, jnp.concatenate(value_grads, 0), 0.0)
            if side != head:
                key_own = pltpu.roll(key_own, HD, 1)
                value_own = pltpu.roll(value_own, HD, 1)
            key_total = key_own if key_total is None else key_total + key_own
            value_total = value_own if value_total is None else value_total + value_own
        query_grad = jnp.concatenate(query_grads, 0)
        dquery_ref[:, lanes] = (query_grad * cosine + turned_back(query_grad * sine)).astype(
            jnp.bfloat16
        )
    key_total = key_total * score_scale
    dkey_ref[...] = (key_total * cosine + turned_back(key_total * sine)).astype(jnp.bfloat16)
    dvalue_ref[...] = value_total.astype(jnp.bfloat16)


def attention_specs(length):
    pair = 2 * HD
    first_key = HQ * HD // pair
    first_value = first_key + KV * HD // pair
    query_spec = pl.BlockSpec((length, GRP * pair), lambda i: (0, i))
    key_spec = pl.BlockSpec((length, pair), lambda i: (0, first_key + i))
    value_spec = pl.BlockSpec((length, pair), lambda i: (0, first_value + i))
    table_spec = pl.BlockSpec((length, pair), lambda i: (0, 0))
    narrow_spec = pl.BlockSpec((length, pair), lambda i: (0, i))
    return query_spec, key_spec, value_spec, table_spec, narrow_spec


def attend_forward(projected, cosine, sine):
    length = projected.shape[0]
    query_spec, key_spec, value_spec, table_spec, _ = attention_specs(length)
    return pl.pallas_call(
        forward_kernel,
        grid=(KV // 2,),
        in_specs=[query_spec, key_spec, value_spec, table_spec, table_spec],
        out_specs=query_spec,
        out_shape=jax.ShapeDtypeStruct((length, HQ * HD), jnp.bfloat16),
        compiler_params=pltpu.CompilerParams(vmem_limit_bytes=32 * 1024 * 1024),
        cost_estimate=pl.CostEstimate(
            flops=4 * HQ * HD * length * length,
            bytes_accessed=12 * length * HQ * HD,
            transcendentals=HQ * length * length,
        ),
    )(projected, projected, projected, cosine, sine)


def attend_backward(projected, grad_mix, cosine, sine):
    length = projected.shape[0]
    query_spec, key_spec, value_spec, table_spec, narrow_spec = attention_specs(length)
    return pl.pallas_call(
        backward_kernel,
        grid=(KV // 2,),
        in_specs=[query_spec, key_spec, value_spec, query_spec, table_spec, table_spec],
        out_specs=[query_spec, narrow_spec, narrow_spec],
        out_shape=[
            jax.ShapeDtypeStruct((length, HQ * HD), jnp.bfloat16),
            jax.ShapeDtypeStruct((length, KV * HD), jnp.bfloat16),
            jax.ShapeDtypeStruct((length, KV * HD), jnp.bfloat16),
        ],
        compiler_params=pltpu.CompilerParams(vmem_limit_bytes=32 * 1024 * 1024),
        cost_estimate=pl.CostEstimate(
            flops=10 * HQ * HD * length * length,
            bytes_accessed=16 * length * HQ * HD,
            transcendentals=HQ * length * length,
        ),
    )(projected, projected, projected, grad_mix, cosine, sine)


def expert_kernel(
    rows_ref,
    turned_ref,
    cotangent_ref,
    gates_ref,
    gate_ref,
    up_ref,
    down_ref,
    moe_ref,
    grad_rows_ref,
    grad_gates_ref,
    gate_grad_ref,
    up_grad_ref,
    down_grad_ref,
    hidden_scratch,
    gate_scratch,
    up_scratch,
):
    expert = pl.program_id(0)
    own_lane = lax.broadcasted_iota(jnp.int32, (1, 128), 1) == expert
    step = 256

    @pl.when(expert == 0)
    def _():
        moe_ref[...] = jnp.zeros_like(moe_ref)
        grad_rows_ref[...] = jnp.zeros_like(grad_rows_ref)
        grad_gates_ref[...] = jnp.zeros_like(grad_gates_ref)

    def row_tile(place, carry):
        rows = pl.ds(pl.multiple_of(place * step, step), step)
        block = rows_ref[rows, :]
        gate_pre = jnp.dot(block, gate_ref[0], preferred_element_type=jnp.float32)
        up_pre = jnp.dot(block, up_ref[0], preferred_element_type=jnp.float32)
        grad_plain = residual_scale * lanes_dot(cotangent_ref[rows, :], down_ref[0])
        gates = jnp.sum(jnp.where(own_lane, gates_ref[rows, :], 0.0), axis=1, keepdims=True)
        sigmoid_gate = 1.0 / (1.0 + jnp.exp(-gate_pre))
        swish_gate = gate_pre * sigmoid_gate
        hidden = swish_gate * up_pre
        hidden_gated = (gates * hidden).astype(jnp.bfloat16)
        inner = jnp.sum(grad_plain * hidden, axis=1, keepdims=True)
        grad_gates_ref[rows, :] += jnp.where(own_lane, inner, 0.0)
        grad_hidden = gates * grad_plain
        grad_gate = (
            grad_hidden * up_pre * sigmoid_gate * (1.0 + gate_pre * (1.0 - sigmoid_gate))
        ).astype(jnp.bfloat16)
        grad_up = (grad_hidden * swish_gate).astype(jnp.bfloat16)
        hidden_scratch[rows, :] = hidden_gated
        gate_scratch[rows, :] = grad_gate
        up_scratch[rows, :] = grad_up
        moe_ref[rows, :] += jnp.dot(hidden_gated, down_ref[0], preferred_element_type=jnp.float32)
        grad_rows_ref[rows, :] += lanes_dot(grad_gate, gate_ref[0]) + lanes_dot(
            grad_up, up_ref[0]
        )
        return carry

    lax.fori_loop(0, rows_ref.shape[0] // step, row_tile, 0)

    def width_tile(place, carry):
        rows = pl.ds(pl.multiple_of(place * step, step), step)
        block = turned_ref[rows, :]
        gate_grad_ref[0, rows, :] = jnp.dot(
            block, gate_scratch[...], preferred_element_type=jnp.float32
        ).astype(jnp.bfloat16)
        up_grad_ref[0, rows, :] = jnp.dot(
            block, up_scratch[...], preferred_element_type=jnp.float32
        ).astype(jnp.bfloat16)
        return carry

    lax.fori_loop(0, turned_ref.shape[0] // step, width_tile, 0)
    for start in range(0, hidden_scratch.shape[1], step):
        part = rows_dot(hidden_scratch[:, start : start + step], cotangent_ref[...])
        down_grad_ref[0, start : start + step, :] = (residual_scale * part).astype(jnp.bfloat16)


def run_experts(rows, cotangent, gates, gate_weight, up_weight, down_weight):
    length, width = rows.shape
    experts, _, inner = gate_weight.shape
    whole_spec = lambda shape: pl.BlockSpec(
        shape, lambda e: (0, 0), pipeline_mode=pl.Buffered(1)
    )
    total_spec = lambda columns: pl.BlockSpec((length, columns), lambda e: (0, 0))
    wide_spec = pl.BlockSpec((1, width, inner), lambda e: (e, 0, 0))
    tall_spec = pl.BlockSpec((1, inner, width), lambda e: (e, 0, 0))
    padded = jnp.concatenate([gates, jnp.zeros((length, 128 - experts), jnp.float32)], 1)
    return pl.pallas_call(
        expert_kernel,
        grid=(experts,),
        in_specs=[
            whole_spec((length, width)),
            whole_spec((width, length)),
            whole_spec((length, width)),
            whole_spec((length, 128)),
            wide_spec,
            wide_spec,
            tall_spec,
        ],
        out_specs=[
            total_spec(width),
            total_spec(width),
            total_spec(128),
            wide_spec,
            wide_spec,
            tall_spec,
        ],
        out_shape=[
            jax.ShapeDtypeStruct((length, width), jnp.float32),
            jax.ShapeDtypeStruct((length, width), jnp.float32),
            jax.ShapeDtypeStruct((length, 128), jnp.float32),
            jax.ShapeDtypeStruct(gate_weight.shape, jnp.bfloat16),
            jax.ShapeDtypeStruct(up_weight.shape, jnp.bfloat16),
            jax.ShapeDtypeStruct(down_weight.shape, jnp.bfloat16),
        ],
        scratch_shapes=[pltpu.VMEM((length, inner), jnp.bfloat16) for _ in range(3)],
        compiler_params=pltpu.CompilerParams(vmem_limit_bytes=56 * 1024 * 1024),
        cost_estimate=pl.CostEstimate(
            flops=18 * experts * length * width * inner,
            bytes_accessed=12 * experts * width * inner,
            transcendentals=experts * length * inner,
        ),
    )(rows, rows.T, cotangent, padded, gate_weight, up_weight, down_weight)


def shards(
    replicas,
    groups,
    tokens,
    cotangent,
    routes,
    first_gain,
    query_weight,
    key_weight,
    value_weight,
    output_weight,
    second_gain,
    router_weight,
    gate_weight,
    up_weight,
    down_weight,
):
    length = tokens.shape[0]
    local_experts = gate_weight.shape[0]
    query_width = query_weight.shape[1]
    key_width = key_weight.shape[1]
    spare = 128 - E - 2
    wide = jnp.concatenate([query_weight, key_weight, value_weight], 1)
    late = jnp.concatenate(
        [
            output_weight,
            router_weight,
            second_gain[:, None],
            first_gain[:, None],
            jnp.zeros((output_weight.shape[0], spare), jnp.bfloat16),
        ],
        1,
    )
    gain_one = group_gather(first_gain, groups)
    wide_full = gather_rows(wide, replicas, groups)
    late_full = gather_rows(late, replicas, groups)
    routes_all = group_gather(routes, groups)
    cotangent_all = group_gather(cotangent, groups)
    output_width = output_weight.shape[1]
    output_full = late_full[:, :output_width]
    router_full = late_full[:, output_width : output_width + E]
    gain_two = late_full[:, output_width + E]
    tokens_float = tokens.astype(jnp.float32)
    scale_one = lax.rsqrt(jnp.mean(tokens_float * tokens_float, axis=-1, keepdims=True) + norm_eps)
    normed_one = (tokens_float * scale_one * gain_one.astype(jnp.float32)).astype(jnp.bfloat16)
    cosine_table, sine_table = rope_tables(length)
    cosine_pair = jnp.concatenate([cosine_table, cosine_table], 1)
    sine_pair = jnp.concatenate([sine_table, sine_table], 1)
    projected = jnp.dot(normed_one, wide_full, preferred_element_type=jnp.float32)
    attention_mix = attend_forward(projected, cosine_pair, sine_pair)
    attention_out = jnp.dot(attention_mix, output_full, preferred_element_type=jnp.float32)
    resid = tokens_float + residual_scale * attention_out
    scale_two = lax.rsqrt(jnp.mean(resid * resid, axis=-1, keepdims=True) + norm_eps)
    normed_two = (resid * scale_two * gain_two.astype(jnp.float32)).astype(jnp.bfloat16)

    normed_all = group_gather(normed_two, groups)
    logits = jnp.dot(normed_all, router_full, preferred_element_type=jnp.float32)
    chosen = jnp.any(
        routes_all[:, :, None] == jnp.arange(E, dtype=jnp.int32)[None, None, :], axis=1
    )
    shown = jnp.where(chosen, logits, -jnp.inf)
    gates = jax.nn.softmax(shown, axis=-1)
    first_expert = lax.axis_index("group") * local_experts
    gates_local = lax.dynamic_slice_in_dim(gates, first_expert, local_experts, 1)
    chunk = 2 * length
    parts = [
        run_experts(
            normed_all[start : start + chunk],
            cotangent_all[start : start + chunk],
            gates_local[start : start + chunk],
            gate_weight,
            up_weight,
            down_weight,
        )
        for start in range(0, normed_all.shape[0], chunk)
    ]
    moe_part, grad_rows_part, grad_gates = (
        jnp.concatenate([part[place] for part in parts], 0) for place in range(3)
    )
    grad_gates = grad_gates[:, :local_experts]
    gate_sum, up_sum, down_sum = (
        flat_rows(sum(part[place].astype(jnp.float32) for part in parts))
        if len(parts) > 1
        else flat_rows(parts[0][place])
        for place in range(3, 6)
    )
    down_sum = sum_step(down_sum, replicas, 0)
    moe_out = group_scatter(moe_part.astype(jnp.bfloat16), groups).astype(jnp.float32)
    layer_output = (resid + residual_scale * moe_out).astype(jnp.bfloat16)

    grad_chosen = gates_local * grad_gates
    grad_logits = lax.dynamic_update_slice_in_dim(
        jnp.zeros_like(gates), grad_chosen, first_expert, 1
    ) - gates * jnp.sum(grad_chosen, axis=-1, keepdims=True)
    grad_logits = grad_logits.astype(jnp.bfloat16)
    router_part = jnp.einsum(
        "sd,se->de", normed_all, grad_logits, preferred_element_type=jnp.float32
    )
    grad_normed_part = (
        grad_rows_part
        + jnp.einsum("se,de->sd", grad_logits, router_full, preferred_element_type=jnp.float32)
    )
    grad_normed_part, down_sum = lax.optimization_barrier(
        (grad_normed_part.astype(jnp.bfloat16), down_sum)
    )
    down_sum = sum_step(down_sum, replicas, 1)
    gate_sum = sum_step(gate_sum, replicas, 0)
    grad_normed_two = group_scatter(grad_normed_part, groups)
    grad_normed_two, gate_sum = lax.optimization_barrier((grad_normed_two, gate_sum))
    grad_normed_two = grad_normed_two.astype(jnp.float32)
    gate_sum = sum_step(gate_sum, replicas, 1)
    up_sum = sum_step(up_sum, replicas, 0, True)
    grad_out = cotangent.astype(jnp.float32)
    second_part = jnp.sum(grad_normed_two * resid * scale_two, axis=0)
    weighted_two = grad_normed_two * gain_two.astype(jnp.float32)
    grad_resid = (
        grad_out
        + scale_two * weighted_two
        - resid * scale_two**3 * jnp.mean(weighted_two * resid, axis=-1, keepdims=True)
    )
    grad_attention = (residual_scale * grad_resid).astype(jnp.bfloat16)
    output_part = jnp.einsum(
        "sk,sd->kd", attention_mix, grad_attention, preferred_element_type=jnp.float32
    )
    grad_mix = jnp.einsum(
        "sd,kd->sk", grad_attention, output_full, preferred_element_type=jnp.float32
    ).astype(jnp.bfloat16)
    grad_mix, up_sum, down_sum = lax.optimization_barrier((grad_mix, up_sum, down_sum))
    up_sum = sum_step(up_sum, replicas, 1, True)
    down_sum = sum_step(down_sum, replicas, 2)
    grad_wide = jnp.concatenate(
        attend_backward(projected, grad_mix, cosine_pair, sine_pair), 1
    )
    grad_wide, gate_sum, down_sum = lax.optimization_barrier((grad_wide, gate_sum, down_sum))
    gate_sum = sum_step(gate_sum, replicas, 2)
    down_sum = sum_step(down_sum, replicas, 3)
    grad_normed_one = jnp.einsum(
        "sk,dk->sd", grad_wide, wide_full, preferred_element_type=jnp.float32
    )
    first_part = jnp.sum(grad_normed_one * tokens_float * scale_one, axis=0)
    wide_part = jnp.einsum("sd,sk->dk", normed_one, grad_wide, preferred_element_type=jnp.float32)
    small_sum = jnp.concatenate(
        [
            wide_part.astype(jnp.bfloat16),
            output_part.astype(jnp.bfloat16),
            router_part.astype(jnp.bfloat16),
            second_part[:, None].astype(jnp.bfloat16),
            first_part[:, None].astype(jnp.bfloat16),
            jnp.zeros((wide_part.shape[0], spare), jnp.bfloat16),
        ],
        1,
    )
    rows = small_sum.shape[0] // groups
    small_sum = small_sum.reshape(groups, rows, small_sum.shape[1])
    states = [small_sum, up_sum, gate_sum, down_sum]
    places = [0, 2, 3, 4]
    while places[0] < 2 * len(bits_of(replicas)) + 1:
        for which in range(4):
            if which == 0:
                states[0] = small_step(states[0], replicas, groups, places[0])
            elif places[which] < 2 * len(bits_of(replicas)):
                states[which] = sum_step(states[which], replicas, places[which], which == 1)
            places[which] += 1
    small_sum = states[0][0].astype(jnp.float32)
    up_grad = states[1].reshape(up_weight.shape)
    gate_grad = states[2].reshape(gate_weight.shape)
    down_grad = states[3].reshape(down_weight.shape)
    weighted_one = grad_normed_one * gain_one.astype(jnp.float32)
    tokens_grad = (
        grad_resid
        + scale_one * weighted_one
        - tokens_float
        * scale_one**3
        * jnp.mean(weighted_one * tokens_float, axis=-1, keepdims=True)
    )
    wide_width = wide.shape[1]
    tail = wide_width + output_width
    return (
        layer_output,
        tokens_grad,
        small_sum[:, tail + E + 1],
        small_sum[:, :query_width],
        small_sum[:, query_width : query_width + key_width],
        small_sum[:, query_width + key_width : wide_width],
        small_sum[:, wide_width:tail],
        small_sum[:, tail + E],
        small_sum[:, tail : tail + E],
        gate_grad,
        up_grad,
        down_grad,
    )


def solution(mesh):
    return jax.shard_map(
        functools.partial(shards, mesh.shape["replica"], mesh.shape["group"]),
        mesh=mesh,
        in_specs=(
            P(("replica", "group"), None),
            P(("replica", "group"), None),
            P(("replica", "group"), None),
            P("group"),
            P("group", None),
            P("group", None),
            P("group", None),
            P("group", None),
            P("group"),
            P("group", None),
            P("group", None, None),
            P("group", None, None),
            P("group", None, None),
        ),
        out_specs=(
            P(("replica", "group"), None),
            P(("replica", "group"), None),
            P("group"),
            P("group", None),
            P("group", None),
            P("group", None),
            P("group", None),
            P("group"),
            P("group", None),
            P("group", None, None),
            P("group", None, None),
            P("group", None, None),
        ),
        check_vma=False,
    )
```
